32 devices in a mesh: parts: 2 (over y), rot: 4 (over z), batch: 2 (over x), wt: 2 (over core).
Axes of the slice: x: 2, y: 2, z: 4, core: 2. Of those that a mesh axis runs over, the one named last changes fastest.
Arguments:
- features: bfloat16 [4, 64, 8, 64, 256], P(('parts', 'batch'), 'rot', 'wt'), parts along dimension 0, may hold values from -6 to 6
- mix_weight: bfloat16 [3, 256, 256], replicated, may hold values from -0.21875 to 0.21875
- conv_weight: bfloat16 [9, 256, 256], replicated, may hold values from -0.125 to 0.125
- cotangent: bfloat16 [4, 64, 8, 64, 256], P(('parts', 'batch'), 'rot', 'wt'), parts along dimension 0, may hold values from -6 to 6
Outputs:
- output: bfloat16 [4, 64, 8, 64, 256], P(('parts', 'batch'), 'rot', 'wt'), parts along dimension 0
- grad_input: bfloat16 [4, 64, 8, 64, 256], P(('parts', 'batch'), 'rot', 'wt'), parts along dimension 0
- weight_grads: float32 [512, 12, 256], P(('parts', 'batch', 'wt'), None, 'rot'), parts along dimension 0
The draws below stay inside these ranges and needn't reach their ends.
There are 2 independent parts, one for each index of `parts`. The reference program is written for one: setup_inputs(seed, part) draws one part's arguments, and reference() takes and returns one part's arrays. A program takes and returns all parts, laid end to end along the dimension named above; an argument that names none is the same for every part. Nothing has to cross between parts.
All inputs are finite; a program needn't handle non-finite values.
Results may differ from the reference program's by a relative error of at most 0.0055.
Values may be sent and summed in bfloat16 or wider, within the bound.
A program may use at most 128 MiB of HBM per device.

```python
import jax
import jax.numpy as jnp
from jax import lax

C = 256
G = 64
GT = 3
KS = 3
COLS = 64
ROWS = 8
BATCH = 2


def raised(drawn, rng, source, target, blocks, factor):
    def block_of(dim):
        return (jnp.arange(drawn.shape[dim]) // (drawn.shape[dim] // blocks)).reshape((-1,) + (1,) * (drawn.ndim - 1 - dim))

    near = jax.random.permutation(rng, blocks)[block_of(target)]
    second = (block_of(target) + blocks // 2) % blocks
    return jnp.where((block_of(source) == near) | (block_of(source) == second), factor * drawn, drawn)


def levels(stream_key, shape, shards, smallest, high):
    level = 1.0
    for dim, shards_of in shards:
        steps = jax.random.uniform(jax.random.fold_in(jax.random.fold_in(stream_key, 6), dim), (shards_of,), jnp.float32, smallest / len(shards), high / len(shards))
        level = level * jnp.repeat(jnp.exp(steps), shape[dim] // shards_of).reshape((-1,) + (1,) * (len(shape) - 1 - dim))
    return level


def gaussian(stream_key, extent, spread, limit, cuts=(), kind=jnp.bfloat16):
    result = jax.random.normal(stream_key, extent, jnp.float32) * spread
    if len(cuts) > 0:
        result = levels(stream_key, extent, cuts, -0.22, 0.18) * result
    return jnp.clip(result, min=-limit, max=limit).astype(kind)


def noise_with(rng, dims, spread, bound, split, heavy, dtype=jnp.bfloat16):
    array = spread * jax.random.normal(rng, dims, jnp.float32)
    if split:
        array = array * levels(rng, dims, split, -0.22, 0.18)
    return jnp.clip(raised(array, jax.random.fold_in(rng, 3), *heavy), -bound, bound).astype(dtype)


def setup_inputs(seed: int = 0, part: int = 0) -> dict:
    seeds = jax.random.split(jax.random.key(seed), 5)
    part_keys = jax.random.split(jax.random.fold_in(seeds[4], part), 5)
    features = noise_with(part_keys[0], (BATCH, G, ROWS, COLS, C), 1.0, 6.0, ((0, 2), (1, 4), (2, 2)), (1, 4, 4, 2.0))
    mix_weight = gaussian(seeds[1], (GT, C, C), (GT * C) ** -0.5, 0.21875)
    conv_weight = gaussian(seeds[2], (KS * KS, C, C), (KS * KS * C) ** -0.5, 0.125)
    cotangent = noise_with(part_keys[3], (BATCH, G, ROWS, COLS, C), 1.0, 6.0, ((0, 2), (1, 4), (2, 2)), (0, 4, 2, 2.0))
    return dict(features=features, mix_weight=mix_weight, conv_weight=conv_weight, cotangent=cotangent)


def contract_first(left, right):
    return lax.dot_general(left, right, (((0,), (0,)), ((), ())), preferred_element_type=jnp.float32)


def contract_last(left, right):
    return lax.dot_general(left, right, (((1,), (1,)), ((), ())), preferred_element_type=jnp.float32)


def reference(features, mix_weight, conv_weight, cotangent):
    channels = features.shape[-1]
    taps = mix_weight.shape[0]
    all_taps = mix_weight.shape[0] + conv_weight.shape[0]

    def one_sample(grads, inputs):
        sample, cot = inputs
        groups, height, breadth, chans = sample.shape
        cycle_feat = jnp.concatenate([sample[-1:], sample, sample[:1]], axis=0)
        cycle_rows = [cycle_feat[offset:offset + groups].reshape(-1, chans) for offset in range(taps)]
        mixed = jnp.zeros((groups * height * breadth, chans), jnp.float32)
        for offset in range(taps):
            mixed = mixed + jnp.dot(cycle_rows[offset], mix_weight[offset], preferred_element_type=jnp.float32)
        mixed = mixed.astype(jnp.bfloat16).reshape(sample.shape)
        mixed_pad = jnp.pad(mixed, ((0, 0), (1, 1), (1, 1), (0, 0)))
        shifted = [mixed_pad[:, row:row + height, col:col + breadth].reshape(-1, chans) for row in range(3) for col in range(3)]
        active = jnp.zeros((groups * height * breadth, chans), jnp.float32)
        for tap_index in range(9):
            active = active + jnp.dot(shifted[tap_index], conv_weight[tap_index], preferred_element_type=jnp.float32)
        sigma = jax.nn.sigmoid(active)
        feat_flat = sample.reshape(-1, chans).astype(jnp.float32)
        output = (feat_flat + active * sigma).astype(jnp.bfloat16).reshape(sample.shape)
        cot_flat = cot.reshape(-1, chans).astype(jnp.float32)
        slope = (cot_flat * (sigma * (1.0 + active * (1.0 - sigma)))).astype(jnp.bfloat16)
        slope_pad = jnp.pad(slope.reshape(sample.shape), ((0, 0), (1, 1), (1, 1), (0, 0)))
        back = jnp.zeros((groups * height * breadth, chans), jnp.float32)
        for row in range(3):
            for col in range(3):
                piece = slope_pad[:, 2 - row:2 - row + height, 2 - col:2 - col + breadth].reshape(-1, chans)
                back = back + contract_last(piece, conv_weight[3 * row + col])
        mixed_grad = back.astype(jnp.bfloat16)
        grad_block = mixed_grad.reshape(sample.shape)
        grad_cycle = jnp.concatenate([grad_block[-1:], grad_block, grad_block[:1]], axis=0)
        total = cot_flat
        for offset in range(taps):
            piece = grad_cycle[2 - offset:2 - offset + groups].reshape(-1, chans)
            total = total + contract_last(piece, mix_weight[offset])
        grad_input = total.astype(jnp.bfloat16).reshape(sample.shape)
        pieces = [contract_first(mixed_grad, cycle_rows[offset]) for offset in range(taps)]
        pieces = pieces + [contract_first(slope, shifted[tap_index]) for tap_index in range(9)]
        grads = grads + jnp.stack(pieces, axis=1)
        return grads, (output, grad_input)

    start = jnp.zeros((channels, all_taps, channels), jnp.float32)
    grads, outs = lax.scan(one_sample, start, (features, cotangent))
    return outs[0], outs[1], grads
```

```python
import functools

import jax
import jax.numpy as jnp
from jax import lax
from jax.experimental import pallas as pl
from jax.experimental.pallas import tpu as pltpu
from jax.sharding import PartitionSpec as P

MESH = pl.DeviceIdType.MESH
F32 = jnp.float32
BF16 = jnp.bfloat16


def dot(left, right):
    return jnp.dot(left, right, preferred_element_type=F32)


def join_rows(pieces):
    return jnp.concatenate(pieces, axis=0)


def join_lanes(pieces):
    return jnp.concatenate(pieces, axis=1)


def kernel(
    cfg, feat_hbm, mixw_hbm, convw_hbm, cot_hbm, out_ref, gin_ref, wgm_ref, wgc_ref,
    feat, cot, wmix, wconv, wmix_t, wconv_t, mbuf, sbuf, slope_t, mgrad_t, mgrad,
    mix_send, mix_recv, slope_send, slope_recv,
    acc_m, acc_c, s1m, s1c, r1m, r1c, s2m, s2c, r2m, r2c, o2m, o2c, s3m, s3c, r3m, r3c, o3m, o3c,
    load_sem, halo_sem, row_sem, sem1, sem2, sem3,
):
    n, height, breadth, ch, nrot, nbatch = cfg
    size = height * breadth
    chunk = ch // (nbatch * 2)
    width = ch // nrot
    rot = lax.axis_index("rot")
    bat = lax.axis_index("batch")
    wt = lax.axis_index("wt")
    other = 1 - wt
    right, left = lax.rem(rot + 1, nrot), lax.rem(rot + nrot - 1, nrot)

    def load(k, src, dst):
        copy = pltpu.make_async_copy(src, dst, load_sem.at[k])
        copy.start()
        return copy

    load_feat = load(0, feat_hbm, feat.at[pl.ds(size, n * size)])
    load_mix = load(1, mixw_hbm, wmix)
    load_conv = load(2, convw_hbm, wconv)
    load_cot = load(3, cot_hbm, cot)

    barrier = pltpu.get_barrier_semaphore()
    pl.semaphore_signal(barrier, inc=1, device_id={"wt": other}, device_id_type=MESH)
    for d in range(1, nbatch):
        pl.semaphore_signal(
            barrier, inc=1, device_id={"batch": lax.rem(bat + d, nbatch)}, device_id_type=MESH
        )
    for d in range(1, nrot):
        pl.semaphore_signal(
            barrier, inc=1, device_id={"rot": lax.rem(rot + d, nrot)}, device_id_type=MESH
        )
    pl.semaphore_wait(barrier, nbatch + nrot - 1)

    def remote(src, dst, send, recv, axis, index):
        copy = pltpu.make_async_remote_copy(
            src_ref=src, dst_ref=dst, send_sem=send, recv_sem=recv,
            device_id={axis: index}, device_id_type=MESH,
        )
        copy.start()
        return copy

    feat_left = remote(
        feat_hbm.at[pl.ds(0, size)], feat.at[pl.ds((n + 1) * size, size)],
        halo_sem.at[0], halo_sem.at[1], "rot", left,
    )
    feat_right = remote(
        feat_hbm.at[pl.ds((n - 1) * size, size)], feat.at[pl.ds(0, size)],
        halo_sem.at[2], halo_sem.at[3], "rot", right,
    )

    def column(rows):
        return lax.rem(lax.broadcasted_iota(jnp.int32, (rows, ch), 0), breadth)

    def spread(value):
        rows = value.shape[0]
        col = column(rows)
        before = jnp.where(col == 0, 0.0, pltpu.roll(value, 1, 0))
        after = jnp.where(col == breadth - 1, 0.0, pltpu.roll(value, rows - 1, 0))
        return join_lanes([before.astype(BF16), value.astype(BF16), after.astype(BF16)])

    def slot(g):
        return g - 1

    def place(g, at, value, buf, edge_buf):
        buf[g, pl.ds(breadth, size), :] = spread(value)
        low = value[size - breadth :]
        high = value[:breadth]
        edge_buf[at] = jnp.where(wt == 0, low, high).astype(BF16)

    near = (1 - wt) * (height + 1) * breadth
    far = wt * (height + 1) * breadth

    def place_halo(g, at, buf, recv):
        buf[g, pl.ds(pl.multiple_of(near, breadth), breadth), :] = spread(recv[at].astype(F32))
        buf[g, pl.ds(pl.multiple_of(far, breadth), breadth), :] = jnp.zeros((breadth, 3 * ch), BF16)

    def rows_of(g):
        return pl.ds(pl.multiple_of(g * size, size), size)

    def cycle(buf, g):
        return join_lanes([buf[rows_of(g + t), :] for t in range(3)])

    def window(buf, g):
        return join_lanes([buf[g, pl.ds(i * breadth, size), :] for i in range(3)])

    def mix_pair(gs, slots):
        value = dot(join_rows([cycle(feat, g) for g in gs]), wmix[...])
        for k, (g, at) in enumerate(zip(gs, slots)):
            place(g, at, value[k * size : (k + 1) * size], mbuf, mix_send)

    def active_pair(gs, slots):
        value = dot(join_rows([window(mbuf, g) for g in gs]), wconv[...])
        for k, (g, at) in enumerate(zip(gs, slots)):
            active = value[k * size : (k + 1) * size]
            sigma = 0.5 * jnp.tanh(0.5 * active) + 0.5
            out_ref[rows_of(g), :] = (
                feat[rows_of(g + 1), :].astype(F32) + active * sigma
            ).astype(BF16)
            slope = cot[rows_of(g), :].astype(F32) * (sigma * (1.0 + active * (1.0 - sigma)))
            place(g, at, slope, sbuf, slope_send)
            slope_t[g] = slope.astype(BF16).T

    def conv_grad_pair(gs):
        lhs = join_lanes([slope_t[g] for g in gs])
        for i in range(3):
            rhs = join_rows([mbuf[g, pl.ds(i * breadth, size), :] for g in gs])
            acc_c[:, pl.ds(i * 3 * ch, 3 * ch)] += dot(lhs, rhs)

    def back_pair(gs):
        value = dot(join_rows([window(sbuf, g) for g in gs]), wconv_t[...]).astype(BF16)
        for k, g in enumerate(gs):
            part = value[k * size : (k + 1) * size]
            mgrad[rows_of(g + 1), :] = part
            mgrad_t[g] = part.T

    def mix_grad_pair(gs):
        lhs = join_lanes([mgrad_t[g] for g in gs])
        for t in range(3):
            rhs = join_rows([feat[rows_of(g + t), :] for g in gs])
            acc_m[:, pl.ds(t * ch, ch)] += dot(lhs, rhs)

    def input_pair(gs):
        value = dot(join_rows([cycle(mgrad, g) for g in gs]), wmix_t[...])
        for k, g in enumerate(gs):
            gin_ref[rows_of(g), :] = (
                cot[rows_of(g), :].astype(F32) + value[k * size : (k + 1) * size]
            ).astype(BF16)

    edges = (0, n - 1)
    edge_slots = (n - 2, n - 1)

    def interior(body):
        def step(k, carry):
            g = 2 * k + 1
            body(g)
            return carry

        lax.fori_loop(0, (n - 2) // 2, step, 0)

    def start_rows(k, send, recv, edge):
        where = pl.ds(n - 2, 2) if edge else pl.ds(0, n - 2)
        return remote(
            send.at[where], recv.at[where], row_sem.at[2 * k], row_sem.at[2 * k + 1], "wt", other
        )

    def start_first(acc, s1, r1, k):
        for b in range(nbatch):
            start = pl.multiple_of((2 * b + other) * chunk, chunk)
            s1[pl.ds(b * chunk, chunk), :] = acc[pl.ds(start, chunk), :].astype(BF16)
        return remote(s1, r1, sem1.at[2 * k], sem1.at[2 * k + 1], "wt", other)

    def total_first(acc, r1, b):
        start = pl.multiple_of((2 * b + wt) * chunk, chunk)
        place_in = pl.multiple_of(b * chunk, chunk)
        return acc[pl.ds(start, chunk), :] + r1[pl.ds(place_in, chunk), :].astype(F32)

    def start_second(first, acc, r1, s2, r2, o2, k):
        first.wait()
        copies = []
        for d in range(1, nbatch):
            b = lax.rem(bat + d, nbatch)
            s2[d - 1] = total_first(acc, r1, b).astype(BF16)
            copies.append(
                remote(
                    s2.at[d - 1], r2.at[d - 1],
                    sem2.at[k, 2 * d - 2], sem2.at[k, 2 * d - 1], "batch", b,
                )
            )
        o2[...] = total_first(acc, r1, bat)
        return copies

    def start_third(second, o2, r2, s3, r3, o3, k, taps):
        for copy in second:
            copy.wait()
        total = o2[...]
        for d in range(1, nbatch):
            total = total + r2[d - 1].astype(F32)
        for q in range(nrot):
            piece = join_lanes(
                [total[:, t * ch + q * width : t * ch + (q + 1) * width] for t in range(taps)]
            )
            o3[q] = piece
            s3[q] = piece.astype(BF16)
        copies = []
        for d in range(1, nrot):
            q = lax.rem(rot + d, nrot)
            copies.append(
                remote(
                    s3.at[q], r3.at[d - 1], sem3.at[k, 2 * d - 2], sem3.at[k, 2 * d - 1], "rot", q
                )
            )
        return copies

    def finish(third, o3, r3, result):
        for copy in third:
            copy.wait()
        total = o3[rot]
        for d in range(1, nrot):
            total = total + r3[d - 1].astype(F32)
        result[...] = total

    load_mix.wait()
    load_feat.wait()
    interior(lambda g: mix_pair((g, g + 1), (slot(g), slot(g + 1))))
    mix_in = start_rows(0, mix_send, mix_recv, False)

    for k in range(3):
        wmix_t[pl.ds(k * ch, ch), :] = wmix[pl.ds((2 - k) * ch, ch), :].T
    load_conv.wait()
    for k in range(9):
        wconv_t[pl.ds(k * ch, ch), :] = wconv[pl.ds((8 - k) * ch, ch), :].T
    acc_c[...] = jnp.zeros_like(acc_c)
    acc_m[...] = jnp.zeros_like(acc_m)
    load_cot.wait()

    mix_in.wait()

    def forward(g):
        for k in range(2):
            place_halo(g + k, slot(g + k), mbuf, mix_recv)
        active_pair((g, g + 1), (slot(g), slot(g + 1)))

    interior(forward)
    slope_in = start_rows(1, slope_send, slope_recv, False)

    feat_left.wait()
    feat_right.wait()
    mix_pair(edges, edge_slots)
    mix_edge = start_rows(2, mix_send, mix_recv, True)
    interior(lambda g: conv_grad_pair((g, g + 1)))
    mix_edge.wait()
    for g, at in zip(edges, edge_slots):
        place_halo(g, at, mbuf, mix_recv)
    active_pair(edges, edge_slots)
    slope_edge = start_rows(3, slope_send, slope_recv, True)
    conv_grad_pair(edges)
    first_c = start_first(acc_c, s1c, r1c, 0)

    slope_edge.wait()
    for g, at in zip(edges, edge_slots):
        place_halo(g, at, sbuf, slope_recv)
    back_pair(edges)
    grad_left = remote(
        mgrad.at[pl.ds(size, size)], mgrad.at[pl.ds((n + 1) * size, size)],
        halo_sem.at[4], halo_sem.at[5], "rot", left,
    )
    grad_right = remote(
        mgrad.at[pl.ds(n * size, size)], mgrad.at[pl.ds(0, size)],
        halo_sem.at[6], halo_sem.at[7], "rot", right,
    )
    second_c = start_second(first_c, acc_c, r1c, s2c, r2c, o2c, 0)
    slope_in.wait()

    def backward(g):
        for k in range(2):
            place_halo(g + k, slot(g + k), sbuf, slope_recv)
        back_pair((g, g + 1))

    interior(backward)

    def mix_grads(k, carry):
        mix_grad_pair((2 * k, 2 * k + 1))
        return carry

    lax.fori_loop(0, n // 2, mix_grads, 0)
    first_m = start_first(acc_m, s1m, r1m, 1)
    third_c = start_third(second_c, o2c, r2c, s3c, r3c, o3c, 0, 9)
    second_m = start_second(first_m, acc_m, r1m, s2m, r2m, o2m, 1)
    interior(lambda g: input_pair((g, g + 1)))
    third_m = start_third(second_m, o2m, r2m, s3m, r3m, o3m, 1, 3)
    grad_left.wait()
    grad_right.wait()
    input_pair(edges)
    finish(third_c, o3c, r3c, wgc_ref)
    finish(third_m, o3m, r3m, wgm_ref)


def local(cfg, features, mix_weight, conv_weight, cotangent):
    n, height, breadth, ch, nrot, nbatch = cfg
    size = height * breadth
    chunk = ch // (nbatch * 2)
    width = ch // nrot
    rows = n * size
    shape = jax.ShapeDtypeStruct
    vmem = pltpu.VMEM

    def stages(make):
        return [make(3), make(9)]

    scratch = [
        vmem((rows + 2 * size, ch), BF16),
        vmem((rows, ch), BF16),
        vmem((3 * ch, ch), BF16),
        vmem((9 * ch, ch), BF16),
        vmem((3 * ch, ch), BF16),
        vmem((9 * ch, ch), BF16),
        vmem((n, size + 2 * breadth, 3 * ch), BF16),
        vmem((n, size + 2 * breadth, 3 * ch), BF16),
        vmem((n, ch, size), BF16),
        vmem((n, ch, size), BF16),
        vmem((rows + 2 * size, ch), BF16),
    ]
    scratch += [vmem((n, breadth, ch), BF16) for _ in range(4)]
    scratch += stages(lambda t: vmem((ch, t * ch), F32))
    scratch += stages(lambda t: vmem((nbatch * chunk, t * ch), BF16))
    scratch += stages(lambda t: vmem((nbatch * chunk, t * ch), BF16))
    scratch += stages(lambda t: vmem((nbatch - 1, chunk, t * ch), BF16))
    scratch += stages(lambda t: vmem((nbatch - 1, chunk, t * ch), BF16))
    scratch += stages(lambda t: vmem((chunk, t * ch), F32))
    scratch += stages(lambda t: vmem((nrot, chunk, t * width), BF16))
    scratch += stages(lambda t: vmem((nrot - 1, chunk, t * width), BF16))
    scratch += stages(lambda t: vmem((nrot, chunk, t * width), F32))
    dma = pltpu.SemaphoreType.DMA
    scratch += [
        dma((4,)), dma((8,)), dma((8,)), dma((4,)),
        dma((2, 2 * (nbatch - 1))), dma((2, 2 * (nrot - 1))),
    ]
    whole = pl.BlockSpec(memory_space=pltpu.VMEM)
    output, grad_input, grads_mix, grads_conv = pl.pallas_call(
        functools.partial(kernel, cfg),
        out_shape=(
            shape((rows, ch), BF16),
            shape((rows, ch), BF16),
            shape((chunk, 3 * width), F32),
            shape((chunk, 9 * width), F32),
        ),
        in_specs=[pl.BlockSpec(memory_space=pl.ANY)] * 4,
        out_specs=(whole, whole, whole, whole),
        scratch_shapes=scratch,
        compiler_params=pltpu.CompilerParams(
            collective_id=0, has_side_effects=True, vmem_limit_bytes=60 * 2**20
        ),
    )(
        features.reshape(rows, ch),
        mix_weight.reshape(3 * ch, ch),
        conv_weight.reshape(9 * ch, ch),
        cotangent.reshape(rows, ch),
    )
    grads = jnp.concatenate(
        [grads_mix.reshape(chunk, 3, width), grads_conv.reshape(chunk, 9, width)], axis=1
    )
    return output.reshape(features.shape), grad_input.reshape(features.shape), grads


def solution(mesh):
    spec = P(("parts", "batch"), "rot", "wt", None, None)

    def run(features, mix_weight, conv_weight, cotangent):
        nrot, nbatch = mesh.shape["rot"], mesh.shape["batch"]
        cfg = (
            features.shape[1] // nrot,
            features.shape[2] // mesh.shape["wt"],
            features.shape[3],
            features.shape[4],
            nrot,
            nbatch,
        )
        return jax.shard_map(
            functools.partial(local, cfg),
            mesh=mesh,
            in_specs=(spec, P(), P(), spec),
            out_specs=(spec, spec, P(("parts", "batch", "wt"), None, "rot")),
            check_vma=False,
        )(features, mix_weight, conv_weight, cotangent)

    return run
```

```python
import functools

import jax
import jax.numpy as jnp
from jax import lax
from jax.experimental import pallas as pl
from jax.experimental.pallas import tpu as pltpu
from jax.sharding import PartitionSpec as P

MESH = pl.DeviceIdType.MESH
F32 = jnp.float32
BF16 = jnp.bfloat16


def dot(left, right):
    return jnp.dot(left, right, preferred_element_type=F32)


def join_rows(pieces):
    return jnp.concatenate(pieces, axis=0)


def join_lanes(pieces):
    return jnp.concatenate(pieces, axis=1)


def kernel(
    cfg, feat_hbm, mixw_hbm, convw_hbm, cot_hbm, out_hbm, gin_hbm, grads_ref,
    out_ref, gin_ref, feat, cot, wmix, wconv, wmix_t, wconv_t, mbuf, sbuf, slope_t, mgrad_t, mgrad,
    mix_send, mix_recv, slope_send, slope_recv,
    acc_m, acc_c, s1m, s1c, r1m, r1c, s2m, s2c, r2m, r2c, o2m, o2c, s3m, s3c, r3m, r3c, o3m, o3c,
    load_sem, store_sem, halo_sem, row_sem, sem1, sem2, sem3,
):
    n, height, breadth, ch, nrot, nbatch = cfg
    size = height * breadth
    chunk = ch // (nbatch * 2)
    width = ch // nrot
    rot = lax.axis_index("rot")
    bat = lax.axis_index("batch")
    wt = lax.axis_index("wt")
    other = 1 - wt
    right, left = lax.rem(rot + 1, nrot), lax.rem(rot + nrot - 1, nrot)

    def load(k, src, dst):
        copy = pltpu.make_async_copy(src, dst, load_sem.at[k])
        copy.start()
        return copy

    def store(k, src, dst, start, count):
        where = pl.ds(start * size, count * size)
        copy = pltpu.make_async_copy(src.at[where], dst.at[where], store_sem.at[k])
        copy.start()
        return copy

    load_feat = load(0, feat_hbm, feat.at[pl.ds(size, n * size)])
    load_mix = load(1, mixw_hbm, wmix)
    load_conv = load(2, convw_hbm, wconv)
    load_cot = load(3, cot_hbm, cot)

    barrier = pltpu.get_barrier_semaphore()
    pl.semaphore_signal(barrier, inc=1, device_id={"wt": other}, device_id_type=MESH)
    for d in range(1, nbatch):
        pl.semaphore_signal(
            barrier, inc=1, device_id={"batch": lax.rem(bat + d, nbatch)}, device_id_type=MESH
        )
    for d in range(1, nrot):
        pl.semaphore_signal(
            barrier, inc=1, device_id={"rot": lax.rem(rot + d, nrot)}, device_id_type=MESH
        )
    pl.semaphore_wait(barrier, nbatch + nrot - 1)

    def remote(src, dst, send, recv, axis, index):
        copy = pltpu.make_async_remote_copy(
            src_ref=src, dst_ref=dst, send_sem=send, recv_sem=recv,
            device_id={axis: index}, device_id_type=MESH,
        )
        copy.start()
        return copy

    feat_left = remote(
        feat_hbm.at[pl.ds(0, size)], feat.at[pl.ds((n + 1) * size, size)],
        halo_sem.at[0], halo_sem.at[1], "rot", left,
    )
    feat_right = remote(
        feat_hbm.at[pl.ds((n - 1) * size, size)], feat.at[pl.ds(0, size)],
        halo_sem.at[2], halo_sem.at[3], "rot", right,
    )

    def column(rows):
        return lax.rem(lax.broadcasted_iota(jnp.int32, (rows, ch), 0), breadth)

    def spread(value):
        rows = value.shape[0]
        col = column(rows)
        before = jnp.where(col == 0, 0.0, pltpu.roll(value, 1, 0))
        after = jnp.where(col == breadth - 1, 0.0, pltpu.roll(value, rows - 1, 0))
        return join_lanes([before.astype(BF16), value.astype(BF16), after.astype(BF16)])

    def slot(g):
        return g - 1

    def place(g, at, value, buf, edge_buf):
        buf[g, pl.ds(breadth, size), :] = spread(value)
        low = value[size - breadth :]
        high = value[:breadth]
        edge_buf[at] = jnp.where(wt == 0, low, high).astype(BF16)

    near = (1 - wt) * (height + 1) * breadth
    far = wt * (height + 1) * breadth

    def place_halo(g, at, buf, recv):
        buf[g, pl.ds(pl.multiple_of(near, breadth), breadth), :] = spread(recv[at].astype(F32))
        buf[g, pl.ds(pl.multiple_of(far, breadth), breadth), :] = jnp.zeros((breadth, 3 * ch), BF16)

    def place_halos(g, buf, recv):
        for k in range(2):
            place_halo(g + k, slot(g + k), buf, recv)

    def rows_of(g):
        return pl.ds(pl.multiple_of(g * size, size), size)

    def cycle(buf, g):
        return join_lanes([buf[rows_of(g + t), :] for t in range(3)])

    def window(buf, g):
        return join_lanes([buf[g, pl.ds(i * breadth, size), :] for i in range(3)])

    def mix_product(gs):
        return dot(join_rows([cycle(feat, g) for g in gs]), wmix[...])

    def mix_after(gs, slots, value):
        for k, (g, at) in enumerate(zip(gs, slots)):
            place(g, at, value[k * size : (k + 1) * size], mbuf, mix_send)

    def active_product(gs):
        return dot(join_rows([window(mbuf, g) for g in gs]), wconv[...])

    def active_after(gs, slots, value):
        for k, (g, at) in enumerate(zip(gs, slots)):
            active = value[k * size : (k + 1) * size]
            sigma = 0.5 * jnp.tanh(0.5 * active) + 0.5
            out_ref[rows_of(g), :] = (
                feat[rows_of(g + 1), :].astype(F32) + active * sigma
            ).astype(BF16)
            slope = cot[rows_of(g), :].astype(F32) * (sigma * (1.0 + active * (1.0 - sigma)))
            place(g, at, slope, sbuf, slope_send)
            slope_t[g] = slope.astype(BF16).T

    def conv_grad_pair(gs):
        lhs = join_lanes([slope_t[g] for g in gs])
        for i in range(3):
            rhs = join_rows([mbuf[g, pl.ds(i * breadth, size), :] for g in gs])
            acc_c[:, pl.ds(i * 3 * ch, 3 * ch)] += dot(lhs, rhs)

    def back_product(gs):
        return dot(join_rows([window(sbuf, g) for g in gs]), wconv_t[...])

    def back_after(gs, slots, value):
        value = value.astype(BF16)
        for k, g in enumerate(gs):
            part = value[k * size : (k + 1) * size]
            mgrad[rows_of(g + 1), :] = part
            mgrad_t[g] = part.T

    def mix_grad_pair(gs):
        lhs = join_lanes([mgrad_t[g] for g in gs])
        for t in range(3):
            rhs = join_rows([feat[rows_of(g + t), :] for g in gs])
            acc_m[:, pl.ds(t * ch, ch)] += dot(lhs, rhs)

    def input_product(gs):
        return dot(join_rows([cycle(mgrad, g) for g in gs]), wmix_t[...])

    def input_after(gs, slots, value):
        for k, g in enumerate(gs):
            gin_ref[rows_of(g), :] = (
                cot[rows_of(g), :].astype(F32) + value[k * size : (k + 1) * size]
            ).astype(BF16)

    edges = (0, n - 1)
    edge_slots = (n - 2, n - 1)

    def interior(body):
        def step(k, carry):
            g = 2 * k + 1
            body(g)
            return carry

        lax.fori_loop(0, (n - 2) // 2, step, 0)

    def at_ends(product, after):
        after(edges, edge_slots, product(edges))

    pairs = (n - 2) // 2
    third_part = pairs // 3

    def staggered(product, after, begin=0, end=pairs):
        if begin == end:
            return

        def step(k, value):
            g = 2 * k + 1
            following = product((g, g + 1))
            after((g - 2, g - 1), (g - 3, g - 2), value)
            return following

        first = 2 * begin + 1
        value = lax.fori_loop(begin + 1, end, step, product((first, first + 1)))
        last = 2 * end - 1
        after((last, last + 1), (last - 1, last), value)

    def start_rows(k, send, recv, edge):
        where = pl.ds(n - 2, 2) if edge else pl.ds(0, n - 2)
        return remote(
            send.at[where], recv.at[where], row_sem.at[2 * k], row_sem.at[2 * k + 1], "wt", other
        )

    def start_first(acc, s1, r1, k):
        for b in range(nbatch):
            start = pl.multiple_of((2 * b + other) * chunk, chunk)
            s1[pl.ds(b * chunk, chunk), :] = acc[pl.ds(start, chunk), :].astype(BF16)
        return remote(s1, r1, sem1.at[2 * k], sem1.at[2 * k + 1], "wt", other)

    def total_first(acc, r1, b):
        start = pl.multiple_of((2 * b + wt) * chunk, chunk)
        place_in = pl.multiple_of(b * chunk, chunk)
        return acc[pl.ds(start, chunk), :] + r1[pl.ds(place_in, chunk), :].astype(F32)

    def start_second(first, acc, r1, s2, r2, o2, k):
        first.wait()
        copies = []
        for d in range(1, nbatch):
            b = lax.rem(bat + d, nbatch)
            s2[d - 1] = total_first(acc, r1, b).astype(BF16)
            copies.append(
                remote(
                    s2.at[d - 1], r2.at[d - 1],
                    sem2.at[k, 2 * d - 2], sem2.at[k, 2 * d - 1], "batch", b,
                )
            )
        o2[...] = total_first(acc, r1, bat)
        return copies

    def start_third(second, o2, r2, s3, r3, o3, k, taps):
        for copy in second:
            copy.wait()
        total = o2[...]
        for d in range(1, nbatch):
            total = total + r2[d - 1].astype(F32)
        for q in range(nrot):
            piece = join_lanes(
                [total[:, t * ch + q * width : t * ch + (q + 1) * width] for t in range(taps)]
            )
            o3[q] = piece
            s3[q] = piece.astype(BF16)
        copies = []
        for d in range(1, nrot):
            q = lax.rem(rot + d, nrot)
            copies.append(
                remote(
                    s3.at[q], r3.at[d - 1], sem3.at[k, 2 * d - 2], sem3.at[k, 2 * d - 1], "rot", q
                )
            )
        return copies

    def finish(third, o3, r3, base, taps):
        for copy in third:
            copy.wait()
        total = o3[rot]
        for d in range(1, nrot):
            total = total + r3[d - 1].astype(F32)
        for t in range(taps):
            grads_ref[base + t] = total[:, t * width : (t + 1) * width]

    load_mix.wait()
    load_feat.wait()
    staggered(mix_product, mix_after)
    mix_in = start_rows(0, mix_send, mix_recv, False)

    for k in range(3):
        wmix_t[pl.ds(k * ch, ch), :] = wmix[pl.ds((2 - k) * ch, ch), :].T
    load_conv.wait()
    for k in range(9):
        wconv_t[pl.ds(k * ch, ch), :] = wconv[pl.ds((8 - k) * ch, ch), :].T
    acc_c[...] = jnp.zeros_like(acc_c)
    acc_m[...] = jnp.zeros_like(acc_m)
    load_cot.wait()

    mix_in.wait()

    interior(lambda g: place_halos(g, mbuf, mix_recv))
    staggered(active_product, active_after)
    slope_in = start_rows(1, slope_send, slope_recv, False)

    feat_left.wait()
    feat_right.wait()
    at_ends(mix_product, mix_after)
    mix_edge = start_rows(2, mix_send, mix_recv, True)
    interior(lambda g: conv_grad_pair((g, g + 1)))
    mix_edge.wait()
    for g, at in zip(edges, edge_slots):
        place_halo(g, at, mbuf, mix_recv)
    at_ends(active_product, active_after)
    store_out = store(0, out_ref, out_hbm, 0, n)
    slope_edge = start_rows(3, slope_send, slope_recv, True)
    conv_grad_pair(edges)
    first_c = start_first(acc_c, s1c, r1c, 0)

    slope_in.wait()
    interior(lambda g: place_halos(g, sbuf, slope_recv))
    staggered(back_product, back_after, 0, third_part)
    second_c = start_second(first_c, acc_c, r1c, s2c, r2c, o2c, 0)
    slope_edge.wait()
    for g, at in zip(edges, edge_slots):
        place_halo(g, at, sbuf, slope_recv)
    at_ends(back_product, back_after)
    grad_left = remote(
        mgrad.at[pl.ds(size, size)], mgrad.at[pl.ds((n + 1) * size, size)],
        halo_sem.at[4], halo_sem.at[5], "rot", left,
    )
    grad_right = remote(
        mgrad.at[pl.ds(n * size, size)], mgrad.at[pl.ds(0, size)],
        halo_sem.at[6], halo_sem.at[7], "rot", right,
    )
    staggered(back_product, back_after, third_part, pairs)

    def mix_grads(k, carry):
        mix_grad_pair((2 * k, 2 * k + 1))
        return carry

    third_c = start_third(second_c, o2c, r2c, s3c, r3c, o3c, 0, 9)
    lax.fori_loop(0, n // 2, mix_grads, 0)
    first_m = start_first(acc_m, s1m, r1m, 1)
    staggered(input_product, input_after, 0, 2 * third_part)
    second_m = start_second(first_m, acc_m, r1m, s2m, r2m, o2m, 1)
    staggered(input_product, input_after, 2 * third_part, pairs)
    store_in = store(1, gin_ref, gin_hbm, 1, n - 2)
    grad_left.wait()
    grad_right.wait()
    at_ends(input_product, input_after)
    store_ends = [
        store(2, gin_ref, gin_hbm, 0, 1), store(3, gin_ref, gin_hbm, n - 1, 1)
    ]
    third_m = start_third(second_m, o2m, r2m, s3m, r3m, o3m, 1, 3)
    finish(third_c, o3c, r3c, 3, 9)
    store_out.wait()
    store_in.wait()
    for copy in store_ends:
        copy.wait()
    finish(third_m, o3m, r3m, 0, 3)


def local(cfg, features, mix_weight, conv_weight, cotangent):
    n, height, breadth, ch, nrot, nbatch = cfg
    size = height * breadth
    chunk = ch // (nbatch * 2)
    width = ch // nrot
    rows = n * size
    shape = jax.ShapeDtypeStruct
    vmem = pltpu.VMEM

    def stages(make):
        return [make(3), make(9)]

    scratch = [
        vmem((rows, ch), BF16),
        vmem((rows, ch), BF16),
        vmem((rows + 2 * size, ch), BF16),
        vmem((rows, ch), BF16),
        vmem((3 * ch, ch), BF16),
        vmem((9 * ch, ch), BF16),
        vmem((3 * ch, ch), BF16),
        vmem((9 * ch, ch), BF16),
        vmem((n, size + 2 * breadth, 3 * ch), BF16),
        vmem((n, size + 2 * breadth, 3 * ch), BF16),
        vmem((n, ch, size), BF16),
        vmem((n, ch, size), BF16),
        vmem((rows + 2 * size, ch), BF16),
    ]
    scratch += [vmem((n, breadth, ch), BF16) for _ in range(4)]
    scratch += stages(lambda t: vmem((ch, t * ch), F32))
    scratch += stages(lambda t: vmem((nbatch * chunk, t * ch), BF16))
    scratch += stages(lambda t: vmem((nbatch * chunk, t * ch), BF16))
    scratch += stages(lambda t: vmem((nbatch - 1, chunk, t * ch), BF16))
    scratch += stages(lambda t: vmem((nbatch - 1, chunk, t * ch), BF16))
    scratch += stages(lambda t: vmem((chunk, t * ch), F32))
    scratch += stages(lambda t: vmem((nrot, chunk, t * width), BF16))
    scratch += stages(lambda t: vmem((nrot - 1, chunk, t * width), BF16))
    scratch += stages(lambda t: vmem((nrot, chunk, t * width), F32))
    dma = pltpu.SemaphoreType.DMA
    scratch += [
        dma((4,)), dma((4,)), dma((8,)), dma((8,)), dma((4,)),
        dma((2, 2 * (nbatch - 1))), dma((2, 2 * (nrot - 1))),
    ]
    remain = pl.BlockSpec(memory_space=pl.ANY)
    whole = pl.BlockSpec(memory_space=pltpu.VMEM)
    output, grad_input, grads = pl.pallas_call(
        functools.partial(kernel, cfg),
        out_shape=(
            shape((rows, ch), BF16),
            shape((rows, ch), BF16),
            shape((12, chunk, width), F32),
        ),
        in_specs=[remain] * 4,
        out_specs=(remain, remain, whole),
        scratch_shapes=scratch,
        compiler_params=pltpu.CompilerParams(
            collective_id=0, has_side_effects=True, vmem_limit_bytes=60 * 2**20
        ),
    )(
        features.reshape(rows, ch),
        mix_weight.reshape(3 * ch, ch),
        conv_weight.reshape(9 * ch, ch),
        cotangent.reshape(rows, ch),
    )
    grads = jnp.transpose(grads, (1, 0, 2))
    return output.reshape(features.shape), grad_input.reshape(features.shape), grads


def solution(mesh):
    spec = P(("parts", "batch"), "rot", "wt", None, None)

    def run(features, mix_weight, conv_weight, cotangent):
        nrot, nbatch = mesh.shape["rot"], mesh.shape["batch"]
        cfg = (
            features.shape[1] // nrot,
            features.shape[2] // mesh.shape["wt"],
            features.shape[3],
            features.shape[4],
            nrot,
            nbatch,
        )
        return jax.shard_map(
            functools.partial(local, cfg),
            mesh=mesh,
            in_specs=(spec, P(), P(), spec),
            out_specs=(spec, spec, P(("parts", "batch", "wt"), None, "rot")),
            check_vma=False,
        )(features, mix_weight, conv_weight, cotangent)

    return run
```

```python
import functools

import jax
import jax.numpy as jnp
from jax import lax
from jax.experimental import pallas as pl
from jax.experimental.pallas import tpu as pltpu
from jax.sharding import PartitionSpec as P

MESH = pl.DeviceIdType.MESH
F32 = jnp.float32
BF16 = jnp.bfloat16


def dot(left, right):
    return jnp.dot(left, right, preferred_element_type=F32)


def join_rows(pieces):
    return jnp.concatenate(pieces, axis=0)


def join_lanes(pieces):
    return jnp.concatenate(pieces, axis=1)


def kernel(
    cfg, feat_hbm, mixw_hbm, convw_hbm, cot_hbm, out_hbm, gin_hbm, grads_ref,
    out_ref, gin_ref, feat, cot, wmix, wconv, wmix_t, wconv_t, mbuf, sbuf, slope_t, mgrad_t, mgrad,
    mix_send, mix_recv, slope_send, slope_recv,
    acc_m, acc_c, s1m, s1c, r1m, r1c, s2m, s2c, r2m, r2c, o2m, o2c, s3m, s3c, r3m, r3c, o3m, o3c,
    load_sem, store_sem, halo_sem, row_sem, sem1, sem2, sem3,
):
    n, height, breadth, ch, nrot, nbatch = cfg
    size = height * breadth
    chunk = ch // (nbatch * 2)
    width = ch // nrot
    rot = lax.axis_index("rot")
    bat = lax.axis_index("batch")
    wt = lax.axis_index("wt")
    other = 1 - wt
    right, left = lax.rem(rot + 1, nrot), lax.rem(rot + nrot - 1, nrot)

    def load(k, src, dst):
        copy = pltpu.make_async_copy(src, dst, load_sem.at[k])
        copy.start()
        return copy

    def store(k, src, dst, start, count):
        where = pl.ds(start * size, count * size)
        copy = pltpu.make_async_copy(src.at[where], dst.at[where], store_sem.at[k])
        copy.start()
        return copy

    load_feat = load(0, feat_hbm, feat.at[pl.ds(size, n * size)])
    load_mix = load(1, mixw_hbm, wmix)
    load_conv = load(2, convw_hbm, wconv)
    load_cot = load(3, cot_hbm, cot)

    barrier = pltpu.get_barrier_semaphore()
    pl.semaphore_signal(barrier, inc=1, device_id={"wt": other}, device_id_type=MESH)
    for d in range(1, nbatch):
        pl.semaphore_signal(
            barrier, inc=1, device_id={"batch": lax.rem(bat + d, nbatch)}, device_id_type=MESH
        )
    for d in range(1, nrot):
        pl.semaphore_signal(
            barrier, inc=1, device_id={"rot": lax.rem(rot + d, nrot)}, device_id_type=MESH
        )
    pl.semaphore_wait(barrier, nbatch + nrot - 1)

    def remote(src, dst, send, recv, axis, index):
        copy = pltpu.make_async_remote_copy(
            src_ref=src, dst_ref=dst, send_sem=send, recv_sem=recv,
            device_id={axis: index}, device_id_type=MESH,
        )
        copy.start()
        return copy

    feat_left = remote(
        feat_hbm.at[pl.ds(0, size)], feat.at[pl.ds((n + 1) * size, size)],
        halo_sem.at[0], halo_sem.at[1], "rot", left,
    )
    feat_right = remote(
        feat_hbm.at[pl.ds((n - 1) * size, size)], feat.at[pl.ds(0, size)],
        halo_sem.at[2], halo_sem.at[3], "rot", right,
    )

    def column(rows):
        return lax.rem(lax.broadcasted_iota(jnp.int32, (rows, ch), 0), breadth)

    def spread(value):
        rows = value.shape[0]
        col = column(rows)
        before = jnp.where(col == 0, 0.0, pltpu.roll(value, 1, 0))
        after = jnp.where(col == breadth - 1, 0.0, pltpu.roll(value, rows - 1, 0))
        return join_lanes([before.astype(BF16), value.astype(BF16), after.astype(BF16)])

    def slot(g):
        return g - 1

    def place(g, at, value, buf, edge_buf):
        buf[g, pl.ds(breadth, size), :] = spread(value)
        low = value[size - breadth :]
        high = value[:breadth]
        edge_buf[at] = jnp.where(wt == 0, low, high).astype(BF16)

    near = (1 - wt) * (height + 1) * breadth
    far = wt * (height + 1) * breadth

    def place_halo(g, at, buf, recv):
        buf[g, pl.ds(pl.multiple_of(near, breadth), breadth), :] = spread(recv[at].astype(F32))
        buf[g, pl.ds(pl.multiple_of(far, breadth), breadth), :] = jnp.zeros((breadth, 3 * ch), BF16)

    def place_halos(g, buf, recv):
        for k in range(2):
            place_halo(g + k, slot(g + k), buf, recv)

    def rows_of(g):
        return pl.ds(pl.multiple_of(g * size, size), size)

    def cycle(buf, g):
        return join_lanes([buf[rows_of(g + t), :] for t in range(3)])

    def window(buf, g):
        return join_lanes([buf[g, pl.ds(i * breadth, size), :] for i in range(3)])

    def mix_product(gs):
        return dot(join_rows([cycle(feat, g) for g in gs]), wmix[...])

    def mix_after(gs, slots, value):
        for k, (g, at) in enumerate(zip(gs, slots)):
            place(g, at, value[k * size : (k + 1) * size], mbuf, mix_send)

    def active_product(gs):
        return dot(join_rows([window(mbuf, g) for g in gs]), wconv[...])

    def active_after(gs, slots, value):
        for k, (g, at) in enumerate(zip(gs, slots)):
            active = value[k * size : (k + 1) * size]
            sigma = 0.5 * jnp.tanh(0.5 * active) + 0.5
            out_ref[rows_of(g), :] = (
                feat[rows_of(g + 1), :].astype(F32) + active * sigma
            ).astype(BF16)
            slope = cot[rows_of(g), :].astype(F32) * (sigma * (1.0 + active * (1.0 - sigma)))
            place(g, at, slope, sbuf, slope_send)
            slope_t[g] = slope.astype(BF16).T

    def conv_grad_pair(gs):
        lhs = join_lanes([slope_t[g] for g in gs])
        for i in range(3):
            rhs = join_rows([mbuf[g, pl.ds(i * breadth, size), :] for g in gs])
            acc_c[:, pl.ds(i * 3 * ch, 3 * ch)] += dot(lhs, rhs)

    def back_product(gs):
        return dot(join_rows([window(sbuf, g) for g in gs]), wconv_t[...])

    def back_after(gs, slots, value):
        value = value.astype(BF16)
        for k, g in enumerate(gs):
            part = value[k * size : (k + 1) * size]
            mgrad[rows_of(g + 1), :] = part
            mgrad_t[g] = part.T

    def mix_grad_pair(gs):
        lhs = join_lanes([mgrad_t[g] for g in gs])
        for t in range(3):
            rhs = join_rows([feat[rows_of(g + t), :] for g in gs])
            acc_m[:, pl.ds(t * ch, ch)] += dot(lhs, rhs)

    def input_product(gs):
        return dot(join_rows([cycle(mgrad, g) for g in gs]), wmix_t[...])

    def input_after(gs, slots, value):
        for k, g in enumerate(gs):
            gin_ref[rows_of(g), :] = (
                cot[rows_of(g), :].astype(F32) + value[k * size : (k + 1) * size]
            ).astype(BF16)

    edges = (0, n - 1)
    edge_slots = (n - 2, n - 1)

    def interior(body):
        def step(k, carry):
            g = 2 * k + 1
            body(g)
            return carry

        lax.fori_loop(0, (n - 2) // 2, step, 0)

    def at_ends(product, after):
        after(edges, edge_slots, product(edges))

    pairs = (n - 2) // 2
    third_part = pairs // 3

    def inner_pairs(product, after, begin=0, end=pairs):
        if begin == end:
            return

        def step(k, carry):
            g = 2 * k + 1
            after((g, g + 1), (slot(g), slot(g + 1)), product((g, g + 1)))
            return carry

        lax.fori_loop(begin, end, step, 0)

    def start_rows(k, send, recv, edge):
        where = pl.ds(n - 2, 2) if edge else pl.ds(0, n - 2)
        return remote(
            send.at[where], recv.at[where], row_sem.at[2 * k], row_sem.at[2 * k + 1], "wt", other
        )

    def start_first(acc, s1, r1, k):
        for b in range(nbatch):
            start = pl.multiple_of((2 * b + other) * chunk, chunk)
            s1[pl.ds(b * chunk, chunk), :] = acc[pl.ds(start, chunk), :].astype(BF16)
        return remote(s1, r1, sem1.at[2 * k], sem1.at[2 * k + 1], "wt", other)

    def total_first(acc, r1, b):
        start = pl.multiple_of((2 * b + wt) * chunk, chunk)
        place_in = pl.multiple_of(b * chunk, chunk)
        return acc[pl.ds(start, chunk), :] + r1[pl.ds(place_in, chunk), :].astype(F32)

    def start_second(first, acc, r1, s2, r2, o2, k):
        first.wait()
        copies = []
        for d in range(1, nbatch):
            b = lax.rem(bat + d, nbatch)
            s2[d - 1] = total_first(acc, r1, b).astype(BF16)
            copies.append(
                remote(
                    s2.at[d - 1], r2.at[d - 1],
                    sem2.at[k, 2 * d - 2], sem2.at[k, 2 * d - 1], "batch", b,
                )
            )
        o2[...] = total_first(acc, r1, bat)
        return copies

    def start_third(second, o2, r2, s3, r3, o3, k, taps):
        for copy in second:
            copy.wait()
        total = o2[...]
        for d in range(1, nbatch):
            total = total + r2[d - 1].astype(F32)
        for q in range(nrot):
            piece = join_lanes(
                [total[:, t * ch + q * width : t * ch + (q + 1) * width] for t in range(taps)]
            )
            o3[q] = piece
            s3[q] = piece.astype(BF16)
        copies = []
        for d in range(1, nrot):
            q = lax.rem(rot + d, nrot)
            copies.append(
                remote(
                    s3.at[q], r3.at[d - 1], sem3.at[k, 2 * d - 2], sem3.at[k, 2 * d - 1], "rot", q
                )
            )
        return copies

    def finish(third, o3, r3, base, taps):
        for copy in third:
            copy.wait()
        total = o3[rot]
        for d in range(1, nrot):
            total = total + r3[d - 1].astype(F32)
        for t in range(taps):
            grads_ref[base + t] = total[:, t * width : (t + 1) * width]

    load_mix.wait()
    load_feat.wait()
    inner_pairs(mix_product, mix_after)
    mix_in = start_rows(0, mix_send, mix_recv, False)

    for k in range(3):
        wmix_t[pl.ds(k * ch, ch), :] = wmix[pl.ds((2 - k) * ch, ch), :].T
    load_conv.wait()
    for k in range(9):
        wconv_t[pl.ds(k * ch, ch), :] = wconv[pl.ds((8 - k) * ch, ch), :].T
    acc_c[...] = jnp.zeros_like(acc_c)
    acc_m[...] = jnp.zeros_like(acc_m)
    load_cot.wait()

    mix_in.wait()

    interior(lambda g: place_halos(g, mbuf, mix_recv))
    inner_pairs(active_product, active_after)
    slope_in = start_rows(1, slope_send, slope_recv, False)

    feat_left.wait()
    feat_right.wait()
    at_ends(mix_product, mix_after)
    mix_edge = start_rows(2, mix_send, mix_recv, True)
    interior(lambda g: conv_grad_pair((g, g + 1)))
    mix_edge.wait()
    for g, at in zip(edges, edge_slots):
        place_halo(g, at, mbuf, mix_recv)
    at_ends(active_product, active_after)
    store_out = store(0, out_ref, out_hbm, 0, n)
    slope_edge = start_rows(3, slope_send, slope_recv, True)
    conv_grad_pair(edges)
    first_c = start_first(acc_c, s1c, r1c, 0)

    slope_in.wait()
    interior(lambda g: place_halos(g, sbuf, slope_recv))
    inner_pairs(back_product, back_after, 0, third_part)
    second_c = start_second(first_c, acc_c, r1c, s2c, r2c, o2c, 0)
    slope_edge.wait()
    for g, at in zip(edges, edge_slots):
        place_halo(g, at, sbuf, slope_recv)
    at_ends(back_product, back_after)
    grad_left = remote(
        mgrad.at[pl.ds(size, size)], mgrad.at[pl.ds((n + 1) * size, size)],
        halo_sem.at[4], halo_sem.at[5], "rot", left,
    )
    grad_right = remote(
        mgrad.at[pl.ds(n * size, size)], mgrad.at[pl.ds(0, size)],
        halo_sem.at[6], halo_sem.at[7], "rot", right,
    )
    inner_pairs(back_product, back_after, third_part, pairs)

    def mix_grads(k, carry):
        mix_grad_pair((2 * k, 2 * k + 1))
        return carry

    third_c = start_third(second_c, o2c, r2c, s3c, r3c, o3c, 0, 9)
    lax.fori_loop(0, n // 2, mix_grads, 0)
    first_m = start_first(acc_m, s1m, r1m, 1)
    inner_pairs(input_product, input_after, 0, 2 * third_part)
    second_m = start_second(first_m, acc_m, r1m, s2m, r2m, o2m, 1)
    inner_pairs(input_product, input_after, 2 * third_part, pairs)
    store_in = store(1, gin_ref, gin_hbm, 1, n - 2)
    grad_left.wait()
    grad_right.wait()
    at_ends(input_product, input_after)
    store_ends = [
        store(2, gin_ref, gin_hbm, 0, 1), store(3, gin_ref, gin_hbm, n - 1, 1)
    ]
    third_m = start_third(second_m, o2m, r2m, s3m, r3m, o3m, 1, 3)
    finish(third_c, o3c, r3c, 3, 9)
    store_out.wait()
    store_in.wait()
    for copy in store_ends:
        copy.wait()
    finish(third_m, o3m, r3m, 0, 3)


def hand_on(*refs):
    count = len(refs) // 2
    for source, target in zip(refs[:count], refs[count:]):
        target[...] = source[...]


def local(cfg, features, mix_weight, conv_weight, cotangent):
    n, height, breadth, ch, nrot, nbatch = cfg
    size = height * breadth
    chunk = ch // (nbatch * 2)
    width = ch // nrot
    rows = n * size
    shape = jax.ShapeDtypeStruct
    vmem = pltpu.VMEM

    def stages(make):
        return [make(3), make(9)]

    scratch = [
        vmem((rows, ch), BF16),
        vmem((rows, ch), BF16),
        vmem((rows + 2 * size, ch), BF16),
        vmem((rows, ch), BF16),
        vmem((3 * ch, ch), BF16),
        vmem((9 * ch, ch), BF16),
        vmem((3 * ch, ch), BF16),
        vmem((9 * ch, ch), BF16),
        vmem((n, size + 2 * breadth, 3 * ch), BF16),
        vmem((n, size + 2 * breadth, 3 * ch), BF16),
        vmem((n, ch, size), BF16),
        vmem((n, ch, size), BF16),
        vmem((rows + 2 * size, ch), BF16),
    ]
    scratch += [vmem((n, breadth, ch), BF16) for _ in range(4)]
    scratch += stages(lambda t: vmem((ch, t * ch), F32))
    scratch += stages(lambda t: vmem((nbatch * chunk, t * ch), BF16))
    scratch += stages(lambda t: vmem((nbatch * chunk, t * ch), BF16))
    scratch += stages(lambda t: vmem((nbatch - 1, chunk, t * ch), BF16))
    scratch += stages(lambda t: vmem((nbatch - 1, chunk, t * ch), BF16))
    scratch += stages(lambda t: vmem((chunk, t * ch), F32))
    scratch += stages(lambda t: vmem((nrot, chunk, t * width), BF16))
    scratch += stages(lambda t: vmem((nrot - 1, chunk, t * width), BF16))
    scratch += stages(lambda t: vmem((nrot, chunk, t * width), F32))
    dma = pltpu.SemaphoreType.DMA
    scratch += [
        dma((4,)), dma((4,)), dma((8,)), dma((8,)), dma((4,)),
        dma((2, 2 * (nbatch - 1))), dma((2, 2 * (nrot - 1))),
    ]
    remain = pl.BlockSpec(memory_space=pl.ANY)
    whole = pl.BlockSpec(memory_space=pltpu.VMEM)
    output, grad_input, grads = pl.pallas_call(
        functools.partial(kernel, cfg),
        out_shape=(
            shape((rows, ch), BF16),
            shape((rows, ch), BF16),
            shape((12, chunk, width), F32),
        ),
        in_specs=[remain] * 4,
        out_specs=(remain, remain, whole),
        scratch_shapes=scratch,
        compiler_params=pltpu.CompilerParams(
            collective_id=0, has_side_effects=True, vmem_limit_bytes=60 * 2**20
        ),
    )(
        features.reshape(rows, ch),
        mix_weight.reshape(3 * ch, ch),
        conv_weight.reshape(9 * ch, ch),
        cotangent.reshape(rows, ch),
    )
    steps = 4
    tile = pl.BlockSpec((rows // steps, ch), lambda i: (i, 0))
    full = pl.BlockSpec((12, chunk, width), lambda i: (0, 0, 0))
    output, grad_input, grads = pl.pallas_call(
        hand_on,
        grid=(steps,),
        out_shape=(
            shape((rows, ch), BF16),
            shape((rows, ch), BF16),
            shape((12, chunk, width), F32),
        ),
        in_specs=[tile, tile, full],
        out_specs=(tile, tile, full),
        compiler_params=pltpu.CompilerParams(vmem_limit_bytes=24 * 2**20),
        cost_estimate=pl.CostEstimate(flops=0, bytes_accessed=8 * rows * ch, transcendentals=0),
    )(output, grad_input, grads)
    grads = jnp.transpose(grads, (1, 0, 2))
    return output.reshape(features.shape), grad_input.reshape(features.shape), grads


def solution(mesh):
    spec = P(("parts", "batch"), "rot", "wt", None, None)

    def run(features, mix_weight, conv_weight, cotangent):
        nrot, nbatch = mesh.shape["rot"], mesh.shape["batch"]
        cfg = (
            features.shape[1] // nrot,
            features.shape[2] // mesh.shape["wt"],
            features.shape[3],
            features.shape[4],
            nrot,
            nbatch,
        )
        return jax.shard_map(
            functools.partial(local, cfg),
            mesh=mesh,
            in_specs=(spec, P(), P(), spec),
            out_specs=(spec, spec, P(("parts", "batch", "wt"), None, "rot")),
            check_vma=False,
        )(features, mix_weight, conv_weight, cotangent)

    return run
```

```python
import functools

import jax
import jax.numpy as jnp
from jax import lax
from jax.experimental import pallas as pl
from jax.experimental.pallas import tpu as pltpu
from jax.sharding import PartitionSpec as P

MESH = pl.DeviceIdType.MESH
F32 = jnp.float32
BF16 = jnp.bfloat16


def dot(left, right):
    return jnp.dot(left, right, preferred_element_type=F32)


def join_rows(pieces):
    return jnp.concatenate(pieces, axis=0)


def join_lanes(pieces):
    return jnp.concatenate(pieces, axis=1)


def kernel(
    cfg, feat_hbm, mixw_hbm, convw_hbm, cot_hbm, out_hbm, gin_hbm, grads_ref,
    out_ref, gin_ref, feat, cot, wmix, wconv, wmix_t, wconv_t, mbuf, sbuf, slope_t, mgrad_t, mgrad,
    mix_send, mix_recv, slope_send, slope_recv,
    acc_m, acc_c, s1m, s1c, r1m, r1c, s2m, s2c, r2m, r2c, o2m, o2c, s3m, s3c, r3m, r3c, o3m, o3c,
    load_sem, store_sem, halo_sem, row_sem, sem1, sem2, sem3,
):
    n, height, breadth, ch, nrot, nbatch = cfg
    size = height * breadth
    chunk = ch // (nbatch * 2)
    width = ch // nrot
    rot = lax.axis_index("rot")
    bat = lax.axis_index("batch")
    wt = lax.axis_index("wt")
    other = 1 - wt
    right, left = lax.rem(rot + 1, nrot), lax.rem(rot + nrot - 1, nrot)

    def load(k, src, dst):
        copy = pltpu.make_async_copy(src, dst, load_sem.at[k])
        copy.start()
        return copy

    def store(k, src, dst, start, count):
        where = pl.ds(start * size, count * size)
        copy = pltpu.make_async_copy(src.at[where], dst.at[where], store_sem.at[k])
        copy.start()
        return copy

    load_feat = load(0, feat_hbm, feat.at[pl.ds(size, n * size)])
    load_mix = load(1, mixw_hbm, wmix)
    load_conv = load(2, convw_hbm, wconv)
    load_cot = load(3, cot_hbm, cot)

    barrier = pltpu.get_barrier_semaphore()
    pl.semaphore_signal(barrier, inc=1, device_id={"wt": other}, device_id_type=MESH)
    for d in range(1, nbatch):
        pl.semaphore_signal(
            barrier, inc=1, device_id={"batch": lax.rem(bat + d, nbatch)}, device_id_type=MESH
        )
    for d in range(1, nrot):
        pl.semaphore_signal(
            barrier, inc=1, device_id={"rot": lax.rem(rot + d, nrot)}, device_id_type=MESH
        )
    pl.semaphore_wait(barrier, nbatch + nrot - 1)

    def remote(src, dst, send, recv, axis, index):
        copy = pltpu.make_async_remote_copy(
            src_ref=src, dst_ref=dst, send_sem=send, recv_sem=recv,
            device_id={axis: index}, device_id_type=MESH,
        )
        copy.start()
        return copy

    feat_left = remote(
        feat_hbm.at[pl.ds(0, size)], feat.at[pl.ds((n + 1) * size, size)],
        halo_sem.at[0], halo_sem.at[1], "rot", left,
    )
    feat_right = remote(
        feat_hbm.at[pl.ds((n - 1) * size, size)], feat.at[pl.ds(0, size)],
        halo_sem.at[2], halo_sem.at[3], "rot", right,
    )

    def column(rows):
        return lax.rem(lax.broadcasted_iota(jnp.int32, (rows, ch), 0), breadth)

    def spread(value):
        rows = value.shape[0]
        col = column(rows)
        before = jnp.where(col == 0, 0.0, pltpu.roll(value, 1, 0))
        after = jnp.where(col == breadth - 1, 0.0, pltpu.roll(value, rows - 1, 0))
        return join_lanes([before.astype(BF16), value.astype(BF16), after.astype(BF16)])

    def slot(g):
        return g - 1

    def place(g, at, value, buf, edge_buf):
        buf[g, pl.ds(breadth, size), :] = spread(value)
        low = value[size - breadth :]
        high = value[:breadth]
        edge_buf[at] = jnp.where(wt == 0, low, high).astype(BF16)

    near = (1 - wt) * (height + 1) * breadth
    far = wt * (height + 1) * breadth

    def place_halo(g, at, buf, recv):
        buf[g, pl.ds(pl.multiple_of(near, breadth), breadth), :] = spread(recv[at].astype(F32))
        buf[g, pl.ds(pl.multiple_of(far, breadth), breadth), :] = jnp.zeros((breadth, 3 * ch), BF16)

    def place_halos(g, buf, recv):
        for k in range(2):
            place_halo(g + k, slot(g + k), buf, recv)

    def rows_of(g):
        return pl.ds(pl.multiple_of(g * size, size), size)

    def cycle(buf, g):
        return join_lanes([buf[rows_of(g + t), :] for t in range(3)])

    def window(buf, g):
        return join_lanes([buf[g, pl.ds(i * breadth, size), :] for i in range(3)])

    def mix_product(gs):
        return dot(join_rows([cycle(feat, g) for g in gs]), wmix[...])

    def mix_after(gs, slots, value):
        for k, (g, at) in enumerate(zip(gs, slots)):
            place(g, at, value[k * size : (k + 1) * size], mbuf, mix_send)

    def active_product(gs):
        return dot(join_rows([window(mbuf, g) for g in gs]), wconv[...])

    def active_after(gs, slots, value):
        for k, (g, at) in enumerate(zip(gs, slots)):
            active = value[k * size : (k + 1) * size]
            sigma = 0.5 * jnp.tanh(0.5 * active) + 0.5
            out_ref[rows_of(g), :] = (
                feat[rows_of(g + 1), :].astype(F32) + active * sigma
            ).astype(BF16)
            slope = cot[rows_of(g), :].astype(F32) * (sigma * (1.0 + active * (1.0 - sigma)))
            place(g, at, slope, sbuf, slope_send)
            slope_t[g] = slope.astype(BF16).T

    def conv_grad_pair(gs):
        lhs = join_lanes([slope_t[g] for g in gs])
        for i in range(3):
            rhs = join_rows([mbuf[g, pl.ds(i * breadth, size), :] for g in gs])
            acc_c[:, pl.ds(i * 3 * ch, 3 * ch)] += dot(lhs, rhs)

    def back_product(gs):
        return dot(join_rows([window(sbuf, g) for g in gs]), wconv_t[...])

    def back_after(gs, slots, value):
        value = value.astype(BF16)
        for k, g in enumerate(gs):
            part = value[k * size : (k + 1) * size]
            mgrad[rows_of(g + 1), :] = part
            mgrad_t[g] = part.T

    def mix_grad_pair(gs):
        lhs = join_lanes([mgrad_t[g] for g in gs])
        for t in range(3):
            rhs = join_rows([feat[rows_of(g + t), :] for g in gs])
            acc_m[:, pl.ds(t * ch, ch)] += dot(lhs, rhs)

    def input_product(gs):
        return dot(join_rows([cycle(mgrad, g) for g in gs]), wmix_t[...])

    def input_after(gs, slots, value):
        for k, g in enumerate(gs):
            gin_ref[rows_of(g), :] = (
                cot[rows_of(g), :].astype(F32) + value[k * size : (k + 1) * size]
            ).astype(BF16)

    edges = (0, n - 1)
    edge_slots = (n - 2, n - 1)

    def interior(body):
        def step(k, carry):
            g = 2 * k + 1
            body(g)
            return carry

        lax.fori_loop(0, (n - 2) // 2, step, 0)

    def at_ends(product, after):
        after(edges, edge_slots, product(edges))

    pairs = (n - 2) // 2
    third_part = pairs // 3

    def inner_pairs(product, after, begin=0, end=pairs):
        if begin == end:
            return

        def step(k, carry):
            g = 2 * k + 1
            after((g, g + 1), (slot(g), slot(g + 1)), product((g, g + 1)))
            return carry

        lax.fori_loop(begin, end, step, 0)

    def start_rows(k, send, recv, edge):
        where = pl.ds(n - 2, 2) if edge else pl.ds(0, n - 2)
        return remote(
            send.at[where], recv.at[where], row_sem.at[2 * k], row_sem.at[2 * k + 1], "wt", other
        )

    def start_first(acc, s1, r1, k):
        for b in range(nbatch):
            start = pl.multiple_of((2 * b + other) * chunk, chunk)
            s1[pl.ds(b * chunk, chunk), :] = acc[pl.ds(start, chunk), :].astype(BF16)
        return remote(s1, r1, sem1.at[2 * k], sem1.at[2 * k + 1], "wt", other)

    def total_first(acc, r1, b):
        start = pl.multiple_of((2 * b + wt) * chunk, chunk)
        place_in = pl.multiple_of(b * chunk, chunk)
        return acc[pl.ds(start, chunk), :] + r1[pl.ds(place_in, chunk), :].astype(F32)

    def start_second(first, acc, r1, s2, r2, o2, k):
        first.wait()
        copies = []
        for d in range(1, nbatch):
            b = lax.rem(bat + d, nbatch)
            s2[d - 1] = total_first(acc, r1, b).astype(BF16)
            copies.append(
                remote(
                    s2.at[d - 1], r2.at[d - 1],
                    sem2.at[k, 2 * d - 2], sem2.at[k, 2 * d - 1], "batch", b,
                )
            )
        o2[...] = total_first(acc, r1, bat)
        return copies

    def start_third(second, o2, r2, s3, r3, o3, k, taps):
        for copy in second:
            copy.wait()
        total = o2[...]
        for d in range(1, nbatch):
            total = total + r2[d - 1].astype(F32)
        for q in range(nrot):
            piece = join_lanes(
                [total[:, t * ch + q * width : t * ch + (q + 1) * width] for t in range(taps)]
            )
            o3[q] = piece
            s3[q] = piece.astype(BF16)
        copies = []
        for d in range(1, nrot):
            q = lax.rem(rot + d, nrot)
            copies.append(
                remote(
                    s3.at[q], r3.at[d - 1], sem3.at[k, 2 * d - 2], sem3.at[k, 2 * d - 1], "rot", q
                )
            )
        return copies

    def finish(third, o3, r3, base, taps):
        for copy in third:
            copy.wait()
        total = o3[rot]
        for d in range(1, nrot):
            total = total + r3[d - 1].astype(F32)
        for t in range(taps):
            grads_ref[base + t] = total[:, t * width : (t + 1) * width]

    load_mix.wait()
    load_feat.wait()
    inner_pairs(mix_product, mix_after)
    mix_in = start_rows(0, mix_send, mix_recv, False)

    for k in range(3):
        wmix_t[pl.ds(k * ch, ch), :] = wmix[pl.ds((2 - k) * ch, ch), :].T
    load_conv.wait()
    for k in range(9):
        wconv_t[pl.ds(k * ch, ch), :] = wconv[pl.ds((8 - k) * ch, ch), :].T
    acc_c[...] = jnp.zeros_like(acc_c)
    acc_m[...] = jnp.zeros_like(acc_m)
    load_cot.wait()

    mix_in.wait()

    interior(lambda g: place_halos(g, mbuf, mix_recv))
    inner_pairs(active_product, active_after)
    slope_in = start_rows(1, slope_send, slope_recv, False)

    feat_left.wait()
    feat_right.wait()
    at_ends(mix_product, mix_after)
    mix_edge = start_rows(2, mix_send, mix_recv, True)
    interior(lambda g: conv_grad_pair((g, g + 1)))
    mix_edge.wait()
    for g, at in zip(edges, edge_slots):
        place_halo(g, at, mbuf, mix_recv)
    at_ends(active_product, active_after)
    store_out = store(0, out_ref, out_hbm, 0, n)
    slope_edge = start_rows(3, slope_send, slope_recv, True)
    conv_grad_pair(edges)
    first_c = start_first(acc_c, s1c, r1c, 0)

    slope_in.wait()
    interior(lambda g: place_halos(g, sbuf, slope_recv))
    inner_pairs(back_product, back_after, 0, third_part)
    second_c = start_second(first_c, acc_c, r1c, s2c, r2c, o2c, 0)
    slope_edge.wait()
    for g, at in zip(edges, edge_slots):
        place_halo(g, at, sbuf, slope_recv)
    at_ends(back_product, back_after)
    grad_left = remote(
        mgrad.at[pl.ds(size, size)], mgrad.at[pl.ds((n + 1) * size, size)],
        halo_sem.at[4], halo_sem.at[5], "rot", left,
    )
    grad_right = remote(
        mgrad.at[pl.ds(n * size, size)], mgrad.at[pl.ds(0, size)],
        halo_sem.at[6], halo_sem.at[7], "rot", right,
    )
    inner_pairs(back_product, back_after, third_part, pairs)

    def mix_grads(k, carry):
        mix_grad_pair((2 * k, 2 * k + 1))
        return carry

    third_c = start_third(second_c, o2c, r2c, s3c, r3c, o3c, 0, 9)
    lax.fori_loop(0, n // 2, mix_grads, 0)
    first_m = start_first(acc_m, s1m, r1m, 1)
    inner_pairs(input_product, input_after, 0, 2 * third_part)
    second_m = start_second(first_m, acc_m, r1m, s2m, r2m, o2m, 1)
    inner_pairs(input_product, input_after, 2 * third_part, pairs)
    store_in = store(1, gin_ref, gin_hbm, 1, n - 2)
    grad_left.wait()
    grad_right.wait()
    at_ends(input_product, input_after)
    store_ends = [
        store(2, gin_ref, gin_hbm, 0, 1), store(3, gin_ref, gin_hbm, n - 1, 1)
    ]
    third_m = start_third(second_m, o2m, r2m, s3m, r3m, o3m, 1, 3)
    finish(third_c, o3c, r3c, 3, 9)
    store_out.wait()
    store_in.wait()
    for copy in store_ends:
        copy.wait()
    finish(third_m, o3m, r3m, 0, 3)


def hand_on(*refs):
    count = len(refs) // 2
    for source, target in zip(refs[:count], refs[count:]):
        target[...] = source[...]


def local(cfg, features, mix_weight, conv_weight, cotangent):
    n, height, breadth, ch, nrot, nbatch = cfg
    size = height * breadth
    chunk = ch // (nbatch * 2)
    width = ch // nrot
    rows = n * size
    shape = jax.ShapeDtypeStruct
    vmem = pltpu.VMEM

    def stages(make):
        return [make(3), make(9)]

    scratch = [
        vmem((rows, ch), BF16),
        vmem((rows, ch), BF16),
        vmem((rows + 2 * size, ch), BF16),
        vmem((rows, ch), BF16),
        vmem((3 * ch, ch), BF16),
        vmem((9 * ch, ch), BF16),
        vmem((3 * ch, ch), BF16),
        vmem((9 * ch, ch), BF16),
        vmem((n, size + 2 * breadth, 3 * ch), BF16),
        vmem((n, size + 2 * breadth, 3 * ch), BF16),
        vmem((n, ch, size), BF16),
        vmem((n, ch, size), BF16),
        vmem((rows + 2 * size, ch), BF16),
    ]
    scratch += [vmem((n, breadth, ch), BF16) for _ in range(4)]
    scratch += stages(lambda t: vmem((ch, t * ch), F32))
    scratch += stages(lambda t: vmem((nbatch * chunk, t * ch), BF16))
    scratch += stages(lambda t: vmem((nbatch * chunk, t * ch), BF16))
    scratch += stages(lambda t: vmem((nbatch - 1, chunk, t * ch), BF16))
    scratch += stages(lambda t: vmem((nbatch - 1, chunk, t * ch), BF16))
    scratch += stages(lambda t: vmem((chunk, t * ch), F32))
    scratch += stages(lambda t: vmem((nrot, chunk, t * width), BF16))
    scratch += stages(lambda t: vmem((nrot - 1, chunk, t * width), BF16))
    scratch += stages(lambda t: vmem((nrot, chunk, t * width), F32))
    dma = pltpu.SemaphoreType.DMA
    scratch += [
        dma((4,)), dma((4,)), dma((8,)), dma((8,)), dma((4,)),
        dma((2, 2 * (nbatch - 1))), dma((2, 2 * (nrot - 1))),
    ]
    remain = pl.BlockSpec(memory_space=pl.ANY)
    whole = pl.BlockSpec(memory_space=pltpu.VMEM)
    output, grad_input, grads = pl.pallas_call(
        functools.partial(kernel, cfg),
        out_shape=(
            shape((rows, ch), BF16),
            shape((rows, ch), BF16),
            shape((12, chunk, width), F32),
        ),
        in_specs=[remain] * 4,
        out_specs=(remain, remain, whole),
        scratch_shapes=scratch,
        compiler_params=pltpu.CompilerParams(
            collective_id=0, has_side_effects=True, vmem_limit_bytes=60 * 2**20
        ),
    )(
        features.reshape(rows, ch),
        mix_weight.reshape(3 * ch, ch),
        conv_weight.reshape(9 * ch, ch),
        cotangent.reshape(rows, ch),
    )
    steps = 4
    tile = pl.BlockSpec((rows // steps, ch), lambda i: (i, 0))
    full = pl.BlockSpec((12, chunk, width), lambda i: (0, 0, 0))
    output, grad_input, grads = pl.pallas_call(
        hand_on,
        grid=(steps,),
        out_shape=(
            shape((rows, ch), BF16),
            shape((rows, ch), BF16),
            shape((12, chunk, width), F32),
        ),
        in_specs=[tile, tile, full],
        out_specs=(tile, tile, full),
        compiler_params=pltpu.CompilerParams(vmem_limit_bytes=60 * 2**20),
        cost_estimate=pl.CostEstimate(flops=0, bytes_accessed=8 * rows * ch, transcendentals=0),
    )(output, grad_input, grads)
    grads = jnp.transpose(grads, (1, 0, 2))
    return output.reshape(features.shape), grad_input.reshape(features.shape), grads


def solution(mesh):
    spec = P(("parts", "batch"), "rot", "wt", None, None)

    def run(features, mix_weight, conv_weight, cotangent):
        nrot, nbatch = mesh.shape["rot"], mesh.shape["batch"]
        cfg = (
            features.shape[1] // nrot,
            features.shape[2] // mesh.shape["wt"],
            features.shape[3],
            features.shape[4],
            nrot,
            nbatch,
        )
        return jax.shard_map(
            functools.partial(local, cfg),
            mesh=mesh,
            in_specs=(spec, P(), P(), spec),
            out_specs=(spec, spec, P(("parts", "batch", "wt"), None, "rot")),
            check_vma=False,
        )(features, mix_weight, conv_weight, cotangent)

    return run
```
